128 devices in a mesh: rollout: 16 (over y, x_lo, core), tensor: 8 (over x_hi, z).
Axes of the slice: x: 4 (x_hi: 2, x_lo: 2; x = x_hi * 2 + x_lo), y: 4, z: 4, core: 2. Of those that a mesh axis runs over, the one named last changes fastest.
Arguments:
- inputs: bfloat16 [4, 2048, 8192], P(None, 'rollout', 'tensor'), may hold values from -6 to 6
- w_query: bfloat16 [8192, 4096], P(None, 'tensor'), may hold values from -0.0625 to 0.0625
- w_keyval: bfloat16 [8192, 2, 1024], P(None, None, 'tensor'), may hold values from -0.0625 to 0.0625
- bias_query: float32 [4096], P('tensor'), may hold values from -3 to 3
- bias_keyval: float32 [2, 1024], P(None, 'tensor'), may hold values from -3 to 3
- factor_down: bfloat16 [128, 3, 64, 8192], P(('rollout', 'tensor')), may hold values from -0.0625 to 0.0625
- factor_up: bfloat16 [128, 64, 6144], P(('rollout', 'tensor')), may hold values from -0.75 to 0.75
- cache: bfloat16 [2, 2048, 128, 1024], P(None, 'rollout', None, 'tensor'), may hold values from -384 to 384
- lengths: int32 [2048], P('rollout'), may hold values from 1 to 128, as said below
- owners: int32 [3], replicated, may hold values from 0 to 127
Outputs:
- context: bfloat16 [4, 2048, 4096], P(None, 'rollout', 'tensor')
The draws below stay inside these ranges and needn't reach their ends.
Inputs may be any that keep to these rules, and one draw needn't show every extreme that they name: `lengths`: in every draw one row has length 128.
All inputs are finite; a program needn't handle non-finite values.
Results may differ from the reference program's by a relative error of at most 0.0085.
The reference program's roundings to bfloat16 on the way count: a program that leaves them out, or rounds other values in their place, can miss the bound.
Values may be sent and summed in bfloat16 or wider, within the bound.
A program may use at most 128 MiB of HBM per device.

```python
import math
import jax
import jax.numpy as jnp
from jax import lax

D = 8192
KVH = 8
HD = 128
QHEADS = 32
R = 64
STEPS = 4
ROWS_DEV = 128
CACHE = 128
ROWS = 2048
DEVICES = 128


def draw_cache(key, part):
    key = jax.random.fold_in(key, 11)
    noise_key = jax.random.fold_in(key, 0)
    entries = jnp.clip(jax.random.normal(noise_key, (2, ROWS, CACHE, KVH * HD), jnp.float32), -6.0, 6.0)
    return entries.astype(jnp.bfloat16)


def draw_lengths(key, part):
    key = jax.random.fold_in(key, 23)
    cap_key, block_key, row_key, pick_key = jax.random.split(key, 4)
    block_count = ROWS // ROWS_DEV
    ceilings = jax.random.randint(cap_key, (block_count,), CACHE // 8, CACHE + 1)
    full_block = jax.random.randint(block_key, (), 0, block_count)
    ceilings = jnp.where(jnp.arange(block_count) == full_block, CACHE, ceilings)
    row_ceilings = jnp.repeat(ceilings, ROWS_DEV, total_repeat_length=ROWS)
    raw_values = jax.random.randint(row_key, (ROWS,), 0, CACHE)
    row_lengths = 1 + raw_values % row_ceilings
    full_row = full_block * ROWS_DEV + jax.random.randint(pick_key, (), 0, ROWS_DEV)
    row_lengths = jnp.where(jnp.arange(ROWS) == full_row, CACHE, row_lengths)
    return row_lengths.astype(jnp.int32)


def steps_of(key, shape, cuts, low, high):
    factor_of = 1.0
    for position, blocks in cuts:
        steps = jax.random.uniform(jax.random.fold_in(jax.random.fold_in(key, 6), position), (blocks,), jnp.float32, low / len(cuts), high / len(cuts))
        factor_of = factor_of * jnp.repeat(jnp.exp(steps), shape[position] // blocks).reshape((-1,) + (1,) * (len(shape) - 1 - position))
    return factor_of


def bell_draw(own_key, shape, scale, most, cuts=(), kind=jnp.bfloat16):
    values = jax.random.normal(own_key, shape, jnp.float32) * scale
    if len(cuts) > 0:
        values = steps_of(own_key, shape, cuts, -0.22, 0.18) * values
    return jnp.clip(values, min=-most, max=most).astype(kind)


def setup_inputs(seed: int = 0) -> dict:
    key_list = jax.random.split(jax.random.key(seed), 11)
    return {
        "inputs": bell_draw(key_list[0], (STEPS, ROWS, D), 1.0, 6.0, ((1, 16), (2, 8))),
        "w_query": bell_draw(key_list[1], (D, QHEADS * HD), D ** -0.5, 0.0625, ((1, 8),)),
        "w_keyval": bell_draw(key_list[2], (D, 2, KVH * HD), D ** -0.5, 0.0625, ((2, 8),)),
        "bias_query": bell_draw(key_list[3], (QHEADS * HD,), 0.5, 3.0, ((0, 8),), jnp.float32),
        "bias_keyval": bell_draw(key_list[4], (2, KVH * HD), 0.5, 3.0, ((1, 8),), jnp.float32),
        "factor_down": bell_draw(key_list[5], (DEVICES, 3, R, D), D ** -0.5, 0.0625, ((0, 128),)),
        "factor_up": bell_draw(key_list[6], (DEVICES, R, QHEADS * HD + 2 * KVH * HD), R ** -0.5, 0.75, ((0, 128),)),
        "cache": draw_cache(jax.random.fold_in(key_list[10], 71), 0),
        "lengths": draw_lengths(jax.random.fold_in(key_list[10], 71), 0),
        "owners": jax.random.randint(key_list[9], (3,), 0, DEVICES).astype(jnp.int32),
    }


def rotate(vectors, positions):
    half_size = vectors.shape[-1] // 2
    frequency = jnp.exp(-(jnp.arange(half_size, dtype=jnp.float32) * (2.0 / vectors.shape[-1])) * math.log(1000000.0))
    angles = positions.astype(jnp.float32)[:, None] * frequency[None, :]
    cosine = jnp.cos(angles)[:, None, :]
    sine = jnp.sin(angles)[:, None, :]
    leading = vectors[..., :half_size]
    trailing = vectors[..., half_size:]
    return jnp.concatenate([leading * cosine - trailing * sine, trailing * cosine + leading * sine], axis=-1)

def reference(inputs, w_query, w_keyval, bias_query, bias_keyval, factor_down, factor_up, cache, lengths, owners):
    query_width = QHEADS * HD
    keyval_width = KVH * HD
    span_starts = [0, query_width, query_width + keyval_width]
    span_sizes = [query_width, keyval_width, keyval_width]
    base_parts = [w_query, w_keyval[:, 0], w_keyval[:, 1]]
    merged_parts = []
    for member in range(3):
        owner_id = owners[member].astype(jnp.int32)
        down_part = lax.dynamic_index_in_dim(factor_down, owner_id, 0, keepdims=False)[member]
        up_whole = lax.dynamic_index_in_dim(factor_up, owner_id, 0, keepdims=False)
        up_part = up_whole[:, span_starts[member]:span_starts[member] + span_sizes[member]]
        low_rank = jnp.dot(down_part.T, up_part, preferred_element_type=jnp.float32)
        merged_parts.append((base_parts[member].astype(jnp.float32) + low_rank).astype(jnp.bfloat16))
    merged_query, merged_key, merged_value = merged_parts
    group_size = QHEADS // KVH
    score_scale = 1.0 / math.sqrt(HD)
    block_count = ROWS // ROWS_DEV

    def one_block(block_id):
        first_row = (block_id * ROWS_DEV).astype(jnp.int32)
        block_inputs = lax.dynamic_slice_in_dim(inputs, first_row, ROWS_DEV, 1)
        block_cache = lax.dynamic_slice_in_dim(cache, first_row, ROWS_DEV, 1)
        block_lengths = lax.dynamic_slice_in_dim(lengths, first_row, ROWS_DEV, 0)
        cache_keys = block_cache[0].astype(jnp.float32).reshape(ROWS_DEV, CACHE, KVH, HD)
        cache_values = block_cache[1].astype(jnp.float32).reshape(ROWS_DEV, CACHE, KVH, HD)
        live_mask = jnp.arange(CACHE, dtype=jnp.int32)[None, :] < block_lengths[:, None]
        new_keys = []
        new_values = []
        outputs = []
        for step_index in range(STEPS):
            positions = block_lengths + step_index
            token_rows = block_inputs[step_index]
            queries = jnp.dot(token_rows, merged_query, preferred_element_type=jnp.float32) + bias_query
            queries = rotate(queries.reshape(ROWS_DEV, QHEADS, HD), positions).astype(jnp.bfloat16)
            keys_now = jnp.dot(token_rows, merged_key, preferred_element_type=jnp.float32) + bias_keyval[0]
            keys_now = rotate(keys_now.reshape(ROWS_DEV, KVH, HD), positions).astype(jnp.bfloat16)
            values_now = jnp.dot(token_rows, merged_value, preferred_element_type=jnp.float32) + bias_keyval[1]
            values_now = values_now.reshape(ROWS_DEV, KVH, HD).astype(jnp.bfloat16)
            new_keys.append(keys_now)
            new_values.append(values_now)
            grouped = queries.astype(jnp.float32).reshape(ROWS_DEV, KVH, group_size, HD)
            cached_scores = jnp.einsum('rkgd,rckd->rkgc', grouped, cache_keys) * score_scale
            cached_scores = jnp.where(live_mask[:, None, None, :], cached_scores, -1e+30)
            recent_keys = jnp.stack(new_keys, axis=1).astype(jnp.float32)
            recent_values = jnp.stack(new_values, axis=1).astype(jnp.float32)
            recent_scores = jnp.einsum('rkgd,rskd->rkgs', grouped, recent_keys) * score_scale
            scores = jnp.concatenate([cached_scores, recent_scores], axis=-1)
            row_max = lax.optimization_barrier(jnp.max(scores, axis=-1, keepdims=True))
            weights = jnp.exp(scores - row_max)
            probs = (weights / lax.optimization_barrier(jnp.sum(weights, axis=-1, keepdims=True))).astype(jnp.bfloat16).astype(jnp.float32)
            context = jnp.einsum('rkgc,rckd->rkgd', probs[..., :CACHE], cache_values)
            context = context + jnp.einsum('rkgs,rskd->rkgd', probs[..., CACHE:], recent_values)
            outputs.append(context.reshape(ROWS_DEV, QHEADS * HD).astype(jnp.bfloat16))
        return jnp.stack(outputs)
    stacked = lax.map(one_block, jnp.arange(block_count, dtype=jnp.int32))
    return jnp.transpose(stacked, (1, 0, 2, 3)).reshape(STEPS, ROWS, QHEADS * HD)
```

```python
import functools
import math

import jax
import jax.numpy as jnp
from jax import lax
from jax.experimental import pallas as pl
from jax.experimental.pallas import tpu as pltpu
from jax.sharding import PartitionSpec as P

MESH = pl.DeviceIdType.MESH
HD = 128
STEPS = 4
ROWS = 128
TOK = STEPS * ROWS
D = 8192
PART = 1024
RANK = 64
HALF = RANK // 2
QW = 512
KW = 128
QFULL = 4096
KFULL = 1024
NSEM = 80
CROSS = (512, 640)
BF = jnp.bfloat16
F32 = jnp.float32


def coordinates():
    rollout = lax.axis_index("rollout")
    tensor = lax.axis_index("tensor")
    core = rollout % 2
    x = (tensor // 4) * 2 + (rollout // 2) % 2
    return core, x, rollout // 4, tensor % 4


def device(core, x, y, z):
    return ((y * 2 + x % 2) * 2 + core, (x // 2) * 4 + z)


def gather_merge_project(
    owners_ref,
    x_hbm,
    wq_hbm,
    wkv_hbm,
    down_hbm,
    up_hbm,
    bq_ref,
    bkv_ref,
    len_ref,
    q_ref,
    k_ref,
    v_ref,
    xs,
    wq,
    wkv,
    mkv,
    pay,
    rcore,
    ry,
    yq,
    rz,
    rx,
    fac,
    acc,
    cos_ref,
    sin_ref,
    send,
    recv,
    local,
):
    core, x, y, z = coordinates()
    tensor = (x // 2) * 4 + z
    me = ((y * 2 + x % 2) * 2 + core) * 8 + tensor

    def at(dc=0, dx=0, dy=0, dz=0):
        return device((core + dc) % 2, (x + dx) % 4, (y + dy) % 4, (z + dz) % 4)

    z_up, z_down, z_far = at(dz=1), at(dz=3), at(dz=2)
    x_far = at(dx=2)
    y_up, y_down = at(dy=1), at(dy=3)
    other = at(dc=1)
    partners = [z_up, z_down, z_far, at(dx=1), x_far, at(dx=3), y_up, y_down, other]

    locals_used = [0]

    def fetch(src, dst):
        copy = pltpu.make_async_copy(src, dst, local.at[locals_used[0]])
        locals_used[0] += 1
        copy.start()
        return copy

    ups = []
    for t in range(8):
        ups.append(fetch(up_hbm.at[0, :, pl.ds(t * QW, QW)], pay.at[0, :, pl.ds(t * PART, QW)]))
        for j in range(2):
            ups.append(
                fetch(
                    up_hbm.at[0, :, pl.ds(QFULL + j * KFULL + t * KW, KW)],
                    pay.at[0, :, pl.ds(t * PART + QW + j * KW, KW)],
                )
            )
    downs = [fetch(down_hbm.at[0, m], pay.at[1 + m]) for m in range(3)]

    barrier = pltpu.get_barrier_semaphore()
    for partner in partners:
        pl.semaphore_signal(barrier, inc=1, device_id=partner, device_id_type=MESH)
    pl.semaphore_wait(barrier, len(partners))

    used = [0]

    def put(src, dst, target):
        index = used[0]
        used[0] += 1
        copy = pltpu.make_async_remote_copy(
            src_ref=src,
            dst_ref=dst,
            send_sem=send.at[index],
            recv_sem=recv.at[index],
            device_id=target,
            device_id_type=MESH,
        )
        copy.start()
        return copy

    started = []

    def push(src, target, dst=None):
        copy = put(src, src if dst is None else dst, target)
        started.append(copy)
        return copy

    def chunk(t, h, columns=None):
        if columns is None:
            return xs.at[t, pl.ds(2 * h, 2)]
        return xs.at[t, pl.ds(2 * h, 2), :, pl.ds(columns[0], columns[1] - columns[0])]

    def own(h):
        return x_hbm.at[pl.ds(2 * h, 2)]

    base = (x // 2) * 4
    far_base = 4 - base
    z_prev, z_next, z_opp = (z + 3) % 4, (z + 1) % 4, (z + 2) % 4

    to_up, to_down, to_x = [], [], []
    for h in range(2):
        to_up.append(push(own(h), z_up, chunk(tensor, h)))
        to_down.append(push(own(h), z_down, chunk(tensor, h)))
        to_x.append(push(own(h), x_far, chunk(tensor, h)))
    x_load = fetch(x_hbm, xs.at[tensor])
    wq_load = fetch(wq_hbm, wq)
    wkv_load = fetch(wkv_hbm, wkv)

    lane = lax.broadcasted_iota(jnp.int32, (ROWS, HD), 1)
    frequency = jnp.exp(
        -((lane % (HD // 2)).astype(F32) * (2.0 / HD)) * math.log(1000000.0)
    )
    lengths = jnp.broadcast_to(len_ref[...], (ROWS, HD)).astype(F32).T
    sign = jnp.where(lane < HD // 2, -1.0, 1.0)
    for s in range(STEPS):
        angles = (lengths + float(s)) * frequency
        cos_ref[pl.ds(s * ROWS, ROWS), :] = jnp.cos(angles)
        sin_ref[pl.ds(s * ROWS, ROWS), :] = jnp.sin(angles) * sign

    keep = [(owners_ref[m] == me).astype(F32).astype(BF) for m in range(3)]
    for t in range(8):
        pay[0, :, pl.ds(t * PART + QW + 2 * KW, PART - QW - 2 * KW)] = jnp.zeros(
            (RANK, PART - QW - 2 * KW), BF
        )
    for copy in ups:
        copy.wait()

    def mask_up(t, carry):
        start = pl.multiple_of(t * PART, PART)
        spans = [(0, QW), (QW, KW), (QW + KW, KW)]
        for m, (offset, width) in enumerate(spans):
            columns = pl.ds(start + offset, width)
            pay[0, :, columns] = pay[0, :, columns] * keep[m]
        return carry

    lax.fori_loop(0, 8, mask_up, 0)
    for copy in downs:
        copy.wait()

    def mask_down(m):
        def mask_block(t, carry):
            columns = pl.ds(pl.multiple_of(t * PART, PART), PART)
            pay[1 + m, :, columns] = pay[1 + m, :, columns] * keep[m]
            return carry

        lax.fori_loop(0, 8, mask_block, 0)

    mine = pl.multiple_of(core * HALF, HALF)
    theirs = pl.multiple_of((1 - core) * HALF, HALF)
    rows = pl.ds(mine, HALF)

    def core_send(g):
        return push(pay.at[pl.ds(2 * g, 2), pl.ds(theirs, HALF)], other, rcore.at[pl.ds(2 * g, 2)])

    mask_down(0)
    core_copies = [core_send(0)]
    mask_down(1)
    mask_down(2)
    core_copies.append(core_send(1))

    def quarter(q):
        return pl.ds(pl.multiple_of(q * 2048, 2048), 2048)

    def core_sum(g):
        core_copies[g].wait_recv()

        def add_block(t, carry):
            columns = pl.ds(pl.multiple_of(t * PART, PART), PART)
            for m in (2 * g, 2 * g + 1):
                rcore[m, :, columns] = rcore[m, :, columns] + pay[m, rows, columns]
            return carry

        lax.fori_loop(0, 8, add_block, 0)

    y_opp, y_next, y_prev = (y + 2) % 4, (y + 1) % 4, (y + 3) % 4

    def y_first(g):
        a, b = 2 * g, 2 * g + 1
        first = [
            push(rcore.at[a, :, quarter(y_opp)], y_up, ry.at[g, 0]),
            push(rcore.at[b, :, quarter(y_opp)], y_down, ry.at[g, 1]),
        ]
        raw = [
            push(rcore.at[a, :, quarter(y_prev)], y_down, ry.at[g, 2]),
            push(rcore.at[b, :, quarter(y_next)], y_up, ry.at[g, 3]),
        ]
        return first, raw

    def y_second(g, first):
        a, b = 2 * g, 2 * g + 1
        first[0].wait_recv()
        ry[g, 0] = ry[g, 0] + rcore[a, :, quarter(y_next)]
        up = push(ry.at[g, 0], y_up, ry.at[g, 4])
        first[1].wait_recv()
        ry[g, 1] = ry[g, 1] + rcore[b, :, quarter(y_prev)]
        down = push(ry.at[g, 1], y_down, ry.at[g, 5])
        return up, down

    def y_third(g, raw, combined):
        a, b = 2 * g, 2 * g + 1
        for copy in (*raw, *combined):
            copy.wait_recv()
        yq[a] = rcore[a, :, quarter(y)] + ry[g, 2] + ry[g, 4]
        yq[b] = rcore[b, :, quarter(y)] + ry[g, 3] + ry[g, 5]

    def part_z(zz):
        return pl.ds(pl.multiple_of(zz * 512, 512), 512)

    def span_z(zz):
        return pl.ds(pl.multiple_of(y * 2048 + zz * 512, 512), 512)

    def span_x(xx):
        return pl.ds(pl.multiple_of(y * 2048 + z * 512 + xx * 128, 128), 128)

    def members(g):
        return pl.ds(2 * g, 2)

    def z_reduce_start(g):
        return [
            push(yq.at[members(g), :, part_z((z + d) % 4)], at(dz=d), rz.at[g, d - 1])
            for d in (1, 2, 3)
        ]

    def z_reduce_end(g, copies):
        for copy in copies:
            copy.wait_recv()
        total = yq[members(g), :, part_z(z)]
        for d in range(3):
            total = total + rz[g, d]
        rz[g, 3] = total

    def x_reduce_start(g):
        return [
            push(
                rz.at[g, 3, :, :, pl.ds(pl.multiple_of(((x + d) % 4) * 128, 128), 128)],
                at(dx=d),
                rx.at[g, d - 1],
            )
            for d in (1, 2, 3)
        ]

    def x_reduce_end(g, copies):
        for copy in copies:
            copy.wait_recv()
        total = rz[g, 3, :, :, pl.ds(pl.multiple_of(x * 128, 128), 128)]
        for d in range(3):
            total = total + rx[g, d]
        rx[g, 3] = total

    def x_spread_start(g):
        return [
            push(rx.at[g, 3], at(dx=d), fac.at[members(g), rows, span_x(x)])
            for d in (1, 2, 3)
        ]

    def x_spread_end(g, copies):
        fac[members(g), rows, span_x(x)] = rx[g, 3]
        for copy in copies:
            copy.wait_recv()

    def z_spread_start(g):
        piece = fac.at[members(g), rows, span_z(z)]
        return [push(piece, at(dz=d)) for d in (1, 2, 3)]

    def wait_all(copies):
        for copy in copies:
            copy.wait_recv()

    def y_spread_start(g):
        piece = fac.at[members(g), rows, quarter(y)]
        return [push(piece, y_up), push(piece, y_down), push(piece, other)]

    def y_forward(g, copies):
        copies[0].wait_recv()
        up = push(fac.at[2 * g, rows, quarter(y_prev)], y_up)
        down_core = push(fac.at[members(g), rows, quarter(y_prev)], other)
        copies[1].wait_recv()
        down = push(fac.at[2 * g + 1, rows, quarter(y_next)], y_down)
        up_core = push(fac.at[members(g), rows, quarter(y_next)], other)
        return up, down, down_core, up_core

    def y_last(g, forwards):
        forwards[0].wait_recv()
        forwards[1].wait_recv()
        return push(fac.at[members(g), rows, quarter(y_opp)], other)

    core_sum(0)
    first0, raw0 = y_first(0)
    core_sum(1)
    first1, raw1 = y_first(1)
    comb0 = y_second(0, first0)

    far_slot = far_base + z
    fwd = {}
    to_up[0].wait_recv()
    fwd["z0"] = push(chunk(base + z_prev, 0), z_up)
    fwd["b_prev0"] = push(chunk(base + z_prev, 0, (CROSS[0], PART)), x_far)
    to_down[0].wait_recv()
    fwd["b_next0"] = push(chunk(base + z_next, 0, (CROSS[0], PART)), x_far)
    to_x[0].wait_recv()
    fwd["a_up0"] = push(chunk(far_slot, 0, (0, CROSS[0])), z_up)
    fwd["a_down0"] = push(chunk(far_slot, 0, (0, CROSS[0])), z_down)

    comb1 = y_second(1, first1)
    y_third(0, raw0, comb0)
    zr0 = z_reduce_start(0)
    z_reduce_end(0, zr0)
    xr0 = x_reduce_start(0)
    y_third(1, raw1, comb1)
    zr1 = z_reduce_start(1)
    x_reduce_end(0, xr0)
    xs0 = x_spread_start(0)
    z_reduce_end(1, zr1)
    xr1 = x_reduce_start(1)
    x_spread_end(0, xs0)
    zs0 = z_spread_start(0)

    to_down[1].wait_recv()
    fwd["z1"] = push(chunk(base + z_next, 1), z_down)
    fwd["b_next1"] = push(chunk(base + z_next, 1, (CROSS[1], PART)), x_far)
    to_up[1].wait_recv()
    fwd["b_prev1"] = push(chunk(base + z_prev, 1, (CROSS[1], PART)), x_far)
    to_x[1].wait_recv()
    fwd["a_up1"] = push(chunk(far_slot, 1, (0, CROSS[1])), z_up)
    fwd["a_down1"] = push(chunk(far_slot, 1, (0, CROSS[1])), z_down)

    x_reduce_end(1, xr1)
    xs1 = x_spread_start(1)
    wait_all(zs0)
    ys0 = y_spread_start(0)
    x_spread_end(1, xs1)
    zs1 = z_spread_start(1)
    wait_all(zs1)
    ys1 = y_spread_start(1)

    fwd["z0"].wait_recv()
    fwd["b_opp0"] = push(chunk(base + z_opp, 0, (CROSS[0], PART)), x_far)
    fwd["z1"].wait_recv()
    fwd["b_opp1"] = push(chunk(base + z_opp, 1, (CROSS[1], PART)), x_far)
    yf0 = y_forward(0, ys0)
    yf1 = y_forward(1, ys1)
    fwd["a_up0"].wait_recv()
    fwd["a_opp0"] = push(chunk(far_base + z_prev, 0, (0, CROSS[0])), z_up)
    fwd["a_down1"].wait_recv()
    fwd["a_opp1"] = push(chunk(far_base + z_next, 1, (0, CROSS[1])), z_down)
    core0 = y_last(0, yf0)
    core1 = y_last(1, yf1)
    for copy in (ys0[2], ys1[2], yf0[2], yf0[3], yf1[2], yf1[3], core0, core1):
        copy.wait_recv()
    for name in ("a_down0", "a_up1", "a_opp0", "a_opp1"):
        fwd[name].wait_recv()
    for name in ("b_prev0", "b_next0", "b_prev1", "b_next1", "b_opp0", "b_opp1"):
        fwd[name].wait_recv()
    for copy in started:
        copy.wait_send()

    x_load.wait()
    wq_load.wait()
    wkv_load.wait()
    up_columns = pl.multiple_of(tensor * PART, PART)
    block = 512

    def merge(i, carry):
        ks = pl.ds(pl.multiple_of(i * block, block), block)
        low = lax.dot_general(
            fac[1, :, ks],
            fac[0, :, pl.ds(up_columns, QW)],
            (((0,), (0,)), ((), ())),
            preferred_element_type=F32,
        )
        wq[ks, :] = (wq[ks, :].astype(F32) + low).astype(BF)
        for j in range(2):
            low = lax.dot_general(
                fac[2 + j, :, ks],
                fac[0, :, pl.ds(up_columns + QW + j * KW, KW)],
                (((0,), (0,)), ((), ())),
                preferred_element_type=F32,
            )
            mkv[ks, pl.ds(j * KW, KW)] = (wkv[ks, pl.ds(j * KW, KW)].astype(F32) + low).astype(BF)
        return carry

    lax.fori_loop(0, D // block, merge, 0)
    acc[...] = jnp.zeros_like(acc)

    def project(t, carry):
        ks = pl.ds(pl.multiple_of(t * PART, PART), PART)
        received = xs[t].reshape(TOK, PART)
        acc[:, pl.ds(0, QW)] += jnp.dot(received, wq[ks, :], preferred_element_type=F32)
        acc[:, pl.ds(QW, 2 * KW)] += jnp.dot(received, mkv[ks, :], preferred_element_type=F32)
        return carry

    lax.fori_loop(0, 8, project, 0)

    def rotate(vectors, token_rows):
        return vectors * cos_ref[token_rows, :] + pltpu.roll(vectors, HD // 2, 1) * sin_ref[token_rows, :]

    for s in range(STEPS):
        token_rows = pl.ds(s * ROWS, ROWS)
        for h in range(QW // HD):
            columns = pl.ds(h * HD, HD)
            turned = rotate(acc[token_rows, columns] + bq_ref[:, columns], token_rows)
            q_ref[:, s * 4 + h, :] = turned.astype(BF).astype(F32)
        turned = rotate(acc[token_rows, pl.ds(QW, KW)] + bkv_ref[pl.ds(0, 1), :], token_rows)
        k_ref[s] = turned.astype(BF)
        v_ref[s] = (acc[token_rows, pl.ds(QW + KW, KW)] + bkv_ref[pl.ds(1, 1), :]).astype(BF)


BLOCK = 32


def attend(len_ref, q_ref, k_ref, v_ref, cache_ref, o_ref, recent, recent_probs, context):
    first = pl.program_id(0) * BLOCK
    queries = q_ref[...].reshape(BLOCK * 16, HD).astype(BF)
    keys = k_ref[...].reshape(BLOCK * STEPS, HD)
    scale = 1.0 / math.sqrt(HD)
    scores = (
        lax.dot_general(queries, keys, (((1,), (1,)), ((), ())), preferred_element_type=F32) * scale
    )
    row = lax.broadcasted_iota(jnp.int32, scores.shape, 0)
    lane = lax.broadcasted_iota(jnp.int32, scores.shape, 1)
    valid = (row // 16 == lane % BLOCK) & (lane // BLOCK <= (row // 4) % 4)
    recent[...] = jnp.where(valid, scores, -1e30)
    slots = lax.broadcasted_iota(jnp.int32, (16, HD), 1)

    def one_row(r):
        mine = pl.ds(r * 16, 16)
        q = q_ref[r].astype(BF)
        cached = (
            lax.dot_general(q, cache_ref[0, r], (((1,), (1,)), ((), ())), preferred_element_type=F32)
            * scale
        )
        cached = jnp.where(slots < len_ref[first + r], cached, -1e30)
        fresh = recent[mine, :]
        top = jnp.max(jnp.maximum(cached, fresh), axis=1, keepdims=True)
        cached = jnp.exp(cached - top)
        fresh = jnp.exp(fresh - top)
        total = jnp.sum(cached + fresh, axis=1, keepdims=True)
        recent_probs[mine, :] = (fresh / total).astype(BF)
        context[r] = jnp.dot((cached / total).astype(BF), cache_ref[1, r], preferred_element_type=F32)

    for r in range(BLOCK):
        one_row(r)
    values = v_ref[...].reshape(BLOCK * STEPS, HD)
    context[...] += jnp.dot(recent_probs[...], values, preferred_element_type=F32).reshape(
        BLOCK, 16, HD
    )
    for s in range(STEPS):
        for h in range(4):
            o_ref[s, :, pl.ds(h * HD, HD)] = context[:, s * 4 + h, :].astype(BF)


def body(
    inputs,
    w_query,
    w_keyval,
    bias_query,
    bias_keyval,
    factor_down,
    factor_up,
    cache,
    lengths,
    owners,
):
    any_space = pl.BlockSpec(memory_space=pl.ANY)
    vmem = pl.BlockSpec(memory_space=pltpu.VMEM)
    smem = pl.BlockSpec(memory_space=pltpu.SMEM)
    queries, keys, values = pl.pallas_call(
        gather_merge_project,
        out_shape=(
            jax.ShapeDtypeStruct((ROWS, 16, HD), F32),
            jax.ShapeDtypeStruct((STEPS, ROWS, HD), BF),
            jax.ShapeDtypeStruct((STEPS, ROWS, HD), BF),
        ),
        in_specs=[smem] + [any_space] * 5 + [vmem] * 3,
        out_specs=(vmem, vmem, vmem),
        scratch_shapes=[
            pltpu.VMEM((8, STEPS, ROWS, PART), BF),
            pltpu.VMEM((D, QW), BF),
            pltpu.VMEM((D, 2 * KW), BF),
            pltpu.VMEM((D, 2 * KW), BF),
            pltpu.VMEM((4, RANK, D), BF),
            pltpu.VMEM((4, HALF, D), BF),
            pltpu.VMEM((2, 6, HALF, 2048), BF),
            pltpu.VMEM((4, HALF, 2048), BF),
            pltpu.VMEM((2, 4, 2, HALF, 512), BF),
            pltpu.VMEM((2, 4, 2, HALF, 128), BF),
            pltpu.VMEM((4, RANK, D), BF),
            pltpu.VMEM((TOK, QW + 2 * KW), F32),
            pltpu.VMEM((TOK, HD), F32),
            pltpu.VMEM((TOK, HD), F32),
            pltpu.SemaphoreType.DMA((NSEM,)),
            pltpu.SemaphoreType.DMA((NSEM,)),
            pltpu.SemaphoreType.DMA((32,)),
        ],
        compiler_params=pltpu.CompilerParams(
            collective_id=0, has_side_effects=True, vmem_limit_bytes=56 << 20
        ),
    )(
        owners,
        inputs,
        w_query,
        w_keyval.reshape(D, 2 * KW),
        factor_down,
        factor_up,
        bias_query.reshape(1, QW),
        bias_keyval,
        lengths.reshape(1, ROWS),
    )
    return pl.pallas_call(
        attend,
        grid=(ROWS // BLOCK,),
        out_shape=jax.ShapeDtypeStruct((STEPS, ROWS, QW), BF),
        in_specs=[
            smem,
            pl.BlockSpec((BLOCK, 16, HD), lambda i: (i, 0, 0)),
            pl.BlockSpec((STEPS, BLOCK, HD), lambda i: (0, i, 0)),
            pl.BlockSpec((STEPS, BLOCK, HD), lambda i: (0, i, 0)),
            pl.BlockSpec((2, BLOCK, HD, HD), lambda i: (0, i, 0, 0)),
        ],
        out_specs=pl.BlockSpec((STEPS, BLOCK, QW), lambda i: (0, i, 0)),
        scratch_shapes=[
            pltpu.VMEM((BLOCK * 16, HD), F32),
            pltpu.VMEM((BLOCK * 16, HD), BF),
            pltpu.VMEM((BLOCK, 16, HD), F32),
        ],
        compiler_params=pltpu.CompilerParams(vmem_limit_bytes=32 << 20),
    )(lengths, queries, keys, values, cache)


def solution(mesh):
    placed = (
        P(None, "rollout", "tensor"),
        P(None, "tensor"),
        P(None, None, "tensor"),
        P("tensor"),
        P(None, "tensor"),
        P(("rollout", "tensor"), None, None, None),
        P(("rollout", "tensor"), None, None),
        P(None, "rollout", None, "tensor"),
        P("rollout"),
        P(),
    )
    return jax.shard_map(
        body, mesh=mesh, in_specs=placed, out_specs=P(None, "rollout", "tensor"), check_vma=False
    )
```

```python
import functools
import math

import jax
import jax.numpy as jnp
from jax import lax
from jax.experimental import pallas as pl
from jax.experimental.pallas import tpu as pltpu
from jax.sharding import PartitionSpec as P

MESH = pl.DeviceIdType.MESH
HD = 128
STEPS = 4
ROWS = 128
TOK = STEPS * ROWS
D = 8192
PART = 1024
RANK = 64
HALF = RANK // 2
QW = 512
KW = 128
QFULL = 4096
KFULL = 1024
NSEM = 190
CROSS = (512, 640)
BF = jnp.bfloat16
F32 = jnp.float32


ORDER = [
    ("f_core", 1), ("f_core", 0), ("f_core", 2), ("f_core", 3), ("zu", 2), ("zd", 2), ("xx", 2),
    ("c_tables", 0), ("f_second", 1), ("c_tables", 1), ("c_tables", 2), ("zu", 3), ("zd", 3),
    ("xx", 3), ("c_tables", 3), ("f_second", 0), ("c_split", 0), ("c_split", 1), ("zu", 4),
    ("zd", 4), ("xx", 4), ("c_split", 2), ("f_second", 2), ("c_split", 3), ("zu", 5), ("zd", 5),
    ("xx", 5), ("f_second", 3), ("zu", 6), ("zd", 6), ("xx", 6), ("f_third", 1), ("f_third", 0),
    ("f_third", 2), ("xx", 7), ("f_third", 3), ("zu", 7), ("zd", 7), ("f_ra", 0), ("f_ra", 1),
    ("xx", 8), ("zu", 8), ("zd", 8), ("f_ra", 2), ("zu", 9), ("zd", 9), ("xx", 9), ("xx", 10),
    ("f_ra", 3), ("f_rb", 1), ("f_rb", 0), ("zu", 10), ("zd", 10), ("xx", 11), ("f_rb", 2),
    ("zu", 11), ("zd", 11), ("xx", 12), ("f_rb", 3), ("f_sb", 1), ("zu", 12), ("f_sb", 0),
    ("xx", 13), ("f_sb", 2), ("xx", 14), ("zd", 12), ("f_sb", 3), ("f_sa", 1), ("xx", 15),
    ("zu", 13), ("zd", 13), ("xx", 16), ("xx", 17), ("f_sa", 0), ("zu", 14), ("f_sa", 3),
    ("zd", 14), ("f_sa", 2), ("xx", 18), ("xx", 19), ("f_yf", 1), ("zu", 15), ("xx", 20),
    ("zd", 15), ("xx", 21), ("f_yf", 0), ("zu", 16), ("xx", 22), ("zd", 16), ("xx", 23), ("zu", 17),
    ("zd", 17), ("xx", 24), ("f_yf", 3), ("zu", 18), ("zd", 18), ("xx", 25), ("zu", 19), ("zd", 19),
    ("xx", 26), ("f_yf", 2), ("xx", 27), ("zu", 20), ("f_last", 1), ("f_own", 1), ("f_near", 1),
    ("zd", 20), ("xx", 28), ("zu", 21), ("f_last", 0), ("f_end", 1), ("f_own", 0), ("f_near", 0),
    ("zd", 21), ("xx", 29), ("f_last", 3), ("f_end", 0), ("f_own", 3), ("f_near", 3), ("zu", 22),
    ("xx", 30), ("zd", 22), ("f_last", 2), ("f_own", 2), ("f_near", 2), ("f_end", 3), ("zu", 23),
    ("xx", 31), ("zd", 23), ("x_end", 0), ("x_end", 1), ("f_end", 2), ("c_merge_q", 0),
    ("c_merge_q", 1), ("c_merge_q", 2), ("c_merge_q", 3), ("x_end", 2), ("c_merge_kv", 0),
    ("c_merge_kv", 1), ("c_merge_kv", 2), ("c_merge_kv", 3), ("c_project", 0), ("c_project", 1),
    ("c_project", 2), ("c_project", 3), ("c_project", 4), ("c_project", 5), ("c_project", 6),
    ("c_project", 7),
]


def coordinates():
    rollout = lax.axis_index("rollout")
    tensor = lax.axis_index("tensor")
    core = rollout % 2
    x = (tensor // 4) * 2 + (rollout // 2) % 2
    return core, x, rollout // 4, tensor % 4


def device(core, x, y, z):
    return ((y * 2 + x % 2) * 2 + core, (x // 2) * 4 + z)


def decode(
    owners_ref,
    x_hbm,
    wq_hbm,
    wkv_hbm,
    down_hbm,
    up_hbm,
    bq_ref,
    bkv_ref,
    len_ref,
    rows_ref,
    cache_hbm,
    o_ref,
    q_ref,
    k_ref,
    v_ref,
    cache_ref,
    recent,
    recent_probs,
    probs,
    xs,
    wq,
    wkv,
    mkv,
    pairs,
    upstage,
    held,
    rcore,
    ry,
    yq,
    rz,
    rx,
    fac,
    upkv,
    acc,
    cos_ref,
    sin_ref,
    send,
    recv,
    local,
):
    core, x, y, z = coordinates()
    tensor = (x // 2) * 4 + z
    me = ((y * 2 + x % 2) * 2 + core) * 8 + tensor

    def at(dc=0, dx=0, dy=0, dz=0):
        return device((core + dc) % 2, (x + dx) % 4, (y + dy) % 4, (z + dz) % 4)

    z_up, z_down, z_far = at(dz=1), at(dz=3), at(dz=2)
    x_far = at(dx=2)
    y_up, y_down = at(dy=1), at(dy=3)
    other = at(dc=1)
    partners = [z_up, z_down, z_far, at(dx=1), x_far, at(dx=3), y_up, y_down, other]

    locals_used = [0]

    def fetch(src, dst):
        copy = pltpu.make_async_copy(src, dst, local.at[locals_used[0]])
        locals_used[0] += 1
        copy.start()
        return copy

    mine = pl.multiple_of(core * HALF, HALF)
    theirs = pl.multiple_of((1 - core) * HALF, HALF)
    rows = pl.ds(mine, HALF)

    barrier = pltpu.get_barrier_semaphore()
    for partner in partners:
        pl.semaphore_signal(barrier, inc=1, device_id=partner, device_id_type=MESH)
    ups = []
    for t in range(8):
        ups.append(fetch(up_hbm.at[0, :, pl.ds(t * QW, QW)], upstage.at[:, pl.ds(t * PART, QW)]))
        for j in range(2):
            ups.append(
                fetch(
                    up_hbm.at[0, :, pl.ds(QFULL + j * KFULL + t * KW, KW)],
                    upstage.at[:, pl.ds(t * PART + QW + j * KW, KW)],
                )
            )
    down_load = fetch(down_hbm.at[0, :, rows], held)
    for t in range(8):
        upstage[:, pl.ds(t * PART + QW + 2 * KW, PART - QW - 2 * KW)] = jnp.zeros(
            (RANK, PART - QW - 2 * KW), BF
        )
    pl.semaphore_wait(barrier, len(partners))

    used = [0]

    def put(src, dst, target):
        index = used[0]
        used[0] += 1
        copy = pltpu.make_async_remote_copy(
            src_ref=src,
            dst_ref=dst,
            send_sem=send.at[index],
            recv_sem=recv.at[index],
            device_id=target,
            device_id_type=MESH,
        )
        copy.start()
        return copy

    started = []
    arrived = set()

    def land(copy):
        if id(copy) not in arrived:
            arrived.add(id(copy))
            copy.wait_recv()

    def push(src, target, dst=None):
        copy = put(src, src if dst is None else dst, target)
        started.append(copy)
        return copy

    def chunk(t, p, columns=(0, PART)):
        piece = xs.at[t, p // 2, pl.ds((p % 2) * 64, 64)]
        if columns == (0, PART):
            return piece
        return piece.at[:, pl.ds(columns[0], columns[1] - columns[0])]

    def own(p):
        return x_hbm.at[p // 2, pl.ds((p % 2) * 64, 64)]

    base = (x // 2) * 4
    far_base = 4 - base
    far_slot = far_base + z
    z_prev, z_next, z_opp = (z + 3) % 4, (z + 1) % 4, (z + 2) % 4

    def across(member):
        return push(down_hbm.at[0, member - 1, pl.ds(theirs, HALF)], other, rcore.at[member])

    core_copies = {1: across(1)}

    got = {}

    def near_part(p):
        return (0, CROSS[p % 2])

    def far_part(p):
        return (CROSS[p % 2], PART)

    up_list = [("own", p) for p in range(8)]
    up_list += [("far", p) for p in range(4)] + [("ring", p) for p in range(4)]
    up_list += [("far", p) for p in range(4, 8)] + [("farring", p) for p in range(4)]

    def z_send(direction, i):
        kind, p = up_list[i]
        if direction < 0:
            p = (p + 4) % 8
        target, behind = (z_up, z_prev) if direction > 0 else (z_down, z_next)
        if kind == "own":
            copy = push(own(p), target, chunk(tensor, p))
        elif kind == "far":
            land(got["x", p])
            copy = push(chunk(far_slot, p, near_part(p)), target)
        elif kind == "ring":
            land(got[direction, "own", p])
            copy = push(chunk(base + behind, p), target)
        else:
            land(got[direction, "far", p])
            copy = push(chunk(far_base + behind, p, near_part(p)), target)
        got[direction, kind, p] = copy

    def zu(i):
        z_send(1, i)

    def zd(i):
        z_send(-1, i)

    x_list = [("own", p) for p in (0, 4, 1, 5, 2, 6, 3, 7)]
    for p in range(4):
        x_list += [("prev", p), ("next", p + 4)]
    for p in range(4):
        x_list += [("prev", p + 4), ("next", p)]
    for p in range(4):
        x_list += [("opp", p), ("opp", p + 4)]

    def xx(i):
        kind, p = x_list[i]
        if kind == "own":
            got["x", p] = push(own(p), x_far, chunk(tensor, p))
            return
        if kind == "prev":
            slot, arrival = base + z_prev, got[1, "own", p]
        elif kind == "next":
            slot, arrival = base + z_next, got[-1, "own", p]
        else:
            slot, arrival = base + z_opp, got[1 if p < 4 else -1, "ring", p]
        land(arrival)
        got["x", kind, p] = push(chunk(slot, p, far_part(p)), x_far)

    def x_end(part):
        for p in range(8):
            if part == 0:
                land(got["x", "prev", p])
                land(got[1, "far", p])
            elif part == 1:
                land(got["x", "next", p])
                land(got[-1, "far", p])
            else:
                land(got["x", "opp", p])
                land(got[1 if p < 4 else -1, "farring", p])

    for i in range(2):
        zu(i)
        zd(i)
        xx(i)
    for copy in ups:
        copy.wait()
    core_copies[0] = push(upstage.at[pl.ds(theirs, HALF)], other, rcore.at[0])
    for member in (2, 3):
        core_copies[member] = across(member)
    x_load = fetch(x_hbm, xs.at[tensor])
    wkv_load = fetch(wkv_hbm, wkv)
    wq_load = fetch(wq_hbm, wq)
    cache_load = fetch(cache_hbm, cache_ref)
    down_load.wait()

    def c_tables(s):
        lane = lax.broadcasted_iota(jnp.int32, (ROWS, HD), 1)
        frequency = jnp.exp(
            -((lane % (HD // 2)).astype(F32) * (2.0 / HD)) * math.log(1000000.0)
        )
        lengths = jnp.broadcast_to(len_ref[...], (ROWS, HD)).astype(F32).T
        sign = jnp.where(lane < HD // 2, -1.0, 1.0)
        angles = (lengths + float(s)) * frequency
        cos_ref[pl.ds(s * ROWS, ROWS), :] = jnp.cos(angles)
        sin_ref[pl.ds(s * ROWS, ROWS), :] = jnp.sin(angles) * sign

    me_other = ((y * 2 + x % 2) * 2 + 1 - core) * 8 + tensor
    keep = [(owners_ref[m] == me).astype(F32).astype(BF) for m in range(3)]
    take = [(owners_ref[m] == me_other).astype(F32).astype(BF) for m in range(3)]

    def quarter(q):
        return pl.ds(pl.multiple_of(q * 2048, 2048), 2048)

    y_opp, y_next, y_prev = (y + 2) % 4, (y + 1) % 4, (y + 3) % 4
    low_rows, high_rows = pl.ds(0, HALF // 2), pl.ds(HALF // 2, HALF // 2)
    fac_low = pl.ds(mine, HALF // 2)
    fac_high = pl.ds(pl.multiple_of(mine + HALF // 2, HALF // 2), HALF // 2)
    state = {}

    def f_core(m):
        land(core_copies[m])
        if m == 0:
            spans = [(0, 0, QW), (1, QW, KW), (2, QW + KW, KW)]
        else:
            spans = [(m - 1, 0, PART)]

        def add_block(t, carry):
            start = pl.multiple_of(t * PART, PART)
            for owner, offset, width in spans:
                columns = pl.ds(start + offset, width)
                here = upstage[rows, columns] if m == 0 else held[m - 1, :, columns]
                rcore[m, :, columns] = here * keep[owner] + rcore[m, :, columns] * take[owner]
            return carry

        lax.fori_loop(0, 8, add_block, 0)
        state["first", m] = [
            push(rcore.at[m, low_rows, quarter(y_opp)], y_up, ry.at[m, 0]),
            push(rcore.at[m, high_rows, quarter(y_opp)], y_down, ry.at[m, 1]),
        ]
        state["raw", m] = [
            push(rcore.at[m, low_rows, quarter(y_prev)], y_down, ry.at[m, 2]),
            push(rcore.at[m, high_rows, quarter(y_next)], y_up, ry.at[m, 3]),
        ]

    def f_second(m):
        land(state["first", m][0])
        ry[m, 0] = ry[m, 0] + rcore[m, low_rows, quarter(y_next)]
        state["raw", m].append(push(ry.at[m, 0], y_up, ry.at[m, 4]))
        land(state["first", m][1])
        ry[m, 1] = ry[m, 1] + rcore[m, high_rows, quarter(y_prev)]
        state["raw", m].append(push(ry.at[m, 1], y_down, ry.at[m, 5]))

    def wait_all(copies):
        for copy in copies:
            land(copy)

    def first_at(m, d):
        return at(dz=d) if m % 2 == 0 else at(dx=d)

    def second_at(m, d):
        return at(dx=d) if m % 2 == 0 else at(dz=d)

    def places(m):
        return (z, x) if m % 2 == 0 else (x, z)

    def wide(index):
        return pl.ds(pl.multiple_of(index * 512, 512), 512)

    def narrow(index):
        return pl.ds(pl.multiple_of(index * 128, 128), 128)

    def f_third(m):
        wait_all(state["raw", m])
        yq[m, low_rows] = rcore[m, low_rows, quarter(y)] + ry[m, 2] + ry[m, 4]
        yq[m, high_rows] = rcore[m, high_rows, quarter(y)] + ry[m, 3] + ry[m, 5]
        outer = places(m)[0]
        state["ra", m] = [
            push(yq.at[m, :, wide((outer + d) % 4)], first_at(m, d), rz.at[m, d - 1])
            for d in (1, 2, 3)
        ]

    def f_ra(m):
        wait_all(state["ra", m])
        outer, inner = places(m)
        rz[m, 3] = yq[m, :, wide(outer)] + rz[m, 0] + rz[m, 1] + rz[m, 2]
        state["rb", m] = [
            push(rz.at[m, 3, :, narrow((inner + d) % 4)], second_at(m, d), rx.at[m, d - 1])
            for d in (1, 2, 3)
        ]

    def f_rb(m):
        wait_all(state["rb", m])
        outer, inner = places(m)
        rx[m, 3] = rz[m, 3, :, narrow(inner)] + rx[m, 0] + rx[m, 1] + rx[m, 2]
        span = pl.ds(pl.multiple_of(y * 2048 + outer * 512 + inner * 128, 128), 128)
        state["sb", m] = [
            push(rx.at[m, 3], second_at(m, d), fac.at[m, rows, span]) for d in (1, 2, 3)
        ]
        fac[m, rows, span] = rx[m, 3]

    def f_sb(m):
        wait_all(state["sb", m])
        outer = places(m)[0]
        piece = fac.at[m, rows, pl.ds(pl.multiple_of(y * 2048 + outer * 512, 512), 512)]
        state["sa", m] = [push(piece, first_at(m, d)) for d in (1, 2, 3)]

    def f_sa(m):
        wait_all(state["sa", m])
        piece = fac.at[m, rows, quarter(y)]
        state["ys", m] = [push(piece, y_up), push(piece, y_down), push(piece, other)]

    def f_yf(m):
        land(state["ys", m][0])
        up = push(fac.at[m, fac_low, quarter(y_prev)], y_up)
        down_core = push(fac.at[m, rows, quarter(y_prev)], other)
        land(state["ys", m][1])
        down = push(fac.at[m, fac_high, quarter(y_next)], y_down)
        up_core = push(fac.at[m, rows, quarter(y_next)], other)
        state["yf", m] = [up, down, down_core, up_core]

    def f_last(m):
        wait_all(state["yf", m][:2])
        state["yl", m] = push(fac.at[m, rows, quarter(y_opp)], other)

    def f_own(m):
        land(state["ys", m][2])

    def f_near(m):
        wait_all(state["yf", m][2:])

    def f_end(m):
        land(state["yl", m])

    def c_split(part):
        if part == 0:
            wkv_load.wait()

        def split_pairs(i, carry):
            pairs[...] = wkv[pl.ds(pl.multiple_of(i * 1024, 1024), 1024), :].astype(F32)
            ks = pl.ds(pl.multiple_of(i * 512, 512), 512)
            for j in range(2):
                mkv[ks, pl.ds(j * KW, KW)] = pairs[pl.ds(j, 512, stride=2), :].astype(BF)
            return carry

        lax.fori_loop(part * 4, part * 4 + 4, split_pairs, 0)

    up_columns = pl.multiple_of(tensor * PART, PART)
    block = 512
    quarters = [y, y_prev, y_next, y_opp]

    def c_merge_q(part):
        if part == 0:
            wq_load.wait()

        def merge(i, carry):
            ks = pl.ds(pl.multiple_of(quarters[part] * 2048 + i * block, block), block)
            low = lax.dot_general(
                fac[1, :, ks],
                fac[0, :, pl.ds(up_columns, QW)],
                (((0,), (0,)), ((), ())),
                preferred_element_type=F32,
            )
            wq[ks, :] = (wq[ks, :].astype(F32) + low).astype(BF)
            return carry

        lax.fori_loop(0, 4, merge, 0)

    def c_merge_kv(part):
        if part == 0:
            upkv[...] = jnp.zeros_like(upkv)
            for j in range(2):
                upkv[pl.ds(j * RANK, RANK), pl.ds(j * KW, KW)] = fac[
                    0, :, pl.ds(up_columns + QW + j * KW, KW)
                ]

        def merge(i, carry):
            ks = pl.ds(pl.multiple_of(quarters[part] * 2048 + i * block, block), block)
            low = lax.dot_general(
                fac[pl.ds(2, 2), :, ks].reshape(2 * RANK, block),
                upkv[...],
                (((0,), (0,)), ((), ())),
                preferred_element_type=F32,
            )
            mkv[ks, :] = (mkv[ks, :].astype(F32) + low).astype(BF)
            return carry

        lax.fori_loop(0, 4, merge, 0)

    sources = [
        tensor, base + z_prev, base + z_next, base + z_opp,
        far_slot, far_base + z_prev, far_base + z_next, far_base + z_opp,
    ]

    def c_project(part):
        t = sources[part]
        if part == 0:
            x_load.wait()
        ks = pl.ds(pl.multiple_of(t * PART, PART), PART)
        received = xs[t].reshape(TOK, PART)
        query = jnp.dot(received, wq[ks, :], preferred_element_type=F32)
        keyval = jnp.dot(received, mkv[ks, :], preferred_element_type=F32)
        if part == 0:
            acc[:, pl.ds(0, QW)] = query
            acc[:, pl.ds(QW, 2 * KW)] = keyval
        else:
            acc[:, pl.ds(0, QW)] += query
            acc[:, pl.ds(QW, 2 * KW)] += keyval

    steps = dict(
        f_core=f_core, f_second=f_second, f_third=f_third, f_ra=f_ra, f_rb=f_rb, f_sb=f_sb, f_sa=f_sa,
        f_yf=f_yf, f_last=f_last, f_own=f_own, f_near=f_near, f_end=f_end,
        zu=zu, zd=zd, xx=xx, x_end=x_end, c_tables=c_tables, c_split=c_split, c_merge_q=c_merge_q, c_merge_kv=c_merge_kv,
        c_project=c_project,
    )
    for name, index in ORDER:
        steps[name](index)

    def rotate(vectors, token_rows):
        return vectors * cos_ref[token_rows, :] + pltpu.roll(vectors, HD // 2, 1) * sin_ref[token_rows, :]

    for s in range(STEPS):
        token_rows = pl.ds(s * ROWS, ROWS)
        for h in range(QW // HD):
            columns = pl.ds(h * HD, HD)
            turned = rotate(acc[token_rows, columns] + bq_ref[:, columns], token_rows)
            q_ref[:, s * 4 + h, :] = turned.astype(BF).astype(F32)
        turned = rotate(acc[token_rows, pl.ds(QW, KW)] + bkv_ref[pl.ds(0, 1), :], token_rows)
        k_ref[s] = turned.astype(BF)
        v_ref[s] = (acc[token_rows, pl.ds(QW + KW, KW)] + bkv_ref[pl.ds(1, 1), :]).astype(BF)

    cache_load.wait()

    def attend_block(i, carry):
        attend(
            pl.multiple_of(i * BLOCK, BLOCK), rows_ref, q_ref, k_ref, v_ref, cache_ref, o_ref,
            recent, recent_probs, probs,
        )
        return carry

    lax.fori_loop(0, ROWS // BLOCK, attend_block, 0)
    for copy in started:
        land(copy)
        copy.wait_send()


BLOCK = 32


def attend(first, len_ref, q_ref, k_ref, v_ref, cache_ref, o_ref, recent, recent_probs, probs):
    rows = pl.ds(first, BLOCK)
    queries = q_ref[rows].reshape(BLOCK * 16, HD).astype(BF)
    keys = k_ref[:, rows, :].reshape(BLOCK * STEPS, HD)
    scale = 1.0 / math.sqrt(HD)
    scores = (
        lax.dot_general(queries, keys, (((1,), (1,)), ((), ())), preferred_element_type=F32) * scale
    )
    row = lax.broadcasted_iota(jnp.int32, scores.shape, 0)
    lane = lax.broadcasted_iota(jnp.int32, scores.shape, 1)
    valid = (row // 16 == lane % BLOCK) & (lane // BLOCK <= (row // 4) % 4)
    recent[...] = jnp.where(valid, scores, -1e30)
    slots = lax.broadcasted_iota(jnp.int32, (16, HD), 1)
    for r in range(BLOCK):
        raw = lax.dot_general(
            q_ref[first + r].astype(BF),
            cache_ref[0, first + r],
            (((1,), (1,)), ((), ())),
            preferred_element_type=F32,
        )
        q_ref[first + r] = jnp.where(slots < len_ref[first + r], raw * scale, -1e30)
    for part in range(4):
        group = pl.ds(first + part * BLOCK // 4, BLOCK // 4)
        mine = pl.ds(part * BLOCK * 4, BLOCK * 4)
        cached = q_ref[group].reshape(BLOCK * 4, HD)
        fresh = recent[mine, :]
        top = jnp.max(jnp.maximum(cached, fresh), axis=1, keepdims=True)
        cached = jnp.exp(cached - top)
        fresh = jnp.exp(fresh - top)
        total = jnp.sum(cached + fresh, axis=1, keepdims=True)
        recent_probs[mine, :] = (fresh / total).astype(BF)
        probs[mine, :] = (cached / total).astype(BF)
    for r in range(BLOCK):
        q_ref[first + r] = jnp.dot(
            probs[pl.ds(r * 16, 16), :], cache_ref[1, first + r], preferred_element_type=F32
        )
    values = v_ref[:, rows, :].reshape(BLOCK * STEPS, HD)
    q_ref[rows] += jnp.dot(recent_probs[...], values, preferred_element_type=F32).reshape(
        BLOCK, 16, HD
    )
    for s in range(STEPS):
        for h in range(4):
            o_ref[s, rows, pl.ds(h * HD, HD)] = q_ref[rows, s * 4 + h, :].astype(BF)


def body(
    inputs,
    w_query,
    w_keyval,
    bias_query,
    bias_keyval,
    factor_down,
    factor_up,
    cache,
    lengths,
    owners,
):
    any_space = pl.BlockSpec(memory_space=pl.ANY)
    vmem = pl.BlockSpec(memory_space=pltpu.VMEM)
    smem = pl.BlockSpec(memory_space=pltpu.SMEM)
    return pl.pallas_call(
        decode,
        out_shape=jax.ShapeDtypeStruct((STEPS, ROWS, QW), BF),
        in_specs=[smem] + [any_space] * 5 + [vmem] * 3 + [smem, any_space],
        out_specs=vmem,
        scratch_shapes=[
            pltpu.VMEM((ROWS, 16, HD), F32),
            pltpu.VMEM((STEPS, ROWS, HD), BF),
            pltpu.VMEM((STEPS, ROWS, HD), BF),
            pltpu.VMEM((2, ROWS, HD, HD), BF),
            pltpu.VMEM((BLOCK * 16, HD), F32),
            pltpu.VMEM((BLOCK * 16, HD), BF),
            pltpu.VMEM((BLOCK * 16, HD), BF),
            pltpu.VMEM((8, STEPS, ROWS, PART), BF),
            pltpu.VMEM((D, QW), BF),
            pltpu.VMEM((2 * D, KW), BF),
            pltpu.VMEM((D, 2 * KW), BF),
            pltpu.VMEM((1024, KW), F32),
            pltpu.VMEM((RANK, D), BF),
            pltpu.VMEM((3, HALF, D), BF),
            pltpu.VMEM((4, HALF, D), BF),
            pltpu.VMEM((4, 6, HALF // 2, 2048), BF),
            pltpu.VMEM((4, HALF, 2048), BF),
            pltpu.VMEM((4, 4, HALF, 512), BF),
            pltpu.VMEM((4, 4, HALF, 128), BF),
            pltpu.VMEM((4, RANK, D), BF),
            pltpu.VMEM((2 * RANK, 2 * KW), BF),
            pltpu.VMEM((TOK, QW + 2 * KW), F32),
            pltpu.VMEM((TOK, HD), F32),
            pltpu.VMEM((TOK, HD), F32),
            pltpu.SemaphoreType.DMA((NSEM,)),
            pltpu.SemaphoreType.DMA((NSEM,)),
            pltpu.SemaphoreType.DMA((32,)),
        ],
        compiler_params=pltpu.CompilerParams(
            collective_id=0, has_side_effects=True, vmem_limit_bytes=58 << 20
        ),
    )(
        owners,
        inputs,
        w_query,
        w_keyval.reshape(2 * D, KW),
        factor_down,
        factor_up,
        bias_query.reshape(1, QW),
        bias_keyval,
        lengths.reshape(1, ROWS),
        lengths,
        cache,
    )


def solution(mesh):
    placed = (
        P(None, "rollout", "tensor"),
        P(None, "tensor"),
        P(None, None, "tensor"),
        P("tensor"),
        P(None, "tensor"),
        P(("rollout", "tensor"), None, None, None),
        P(("rollout", "tensor"), None, None),
        P(None, "rollout", None, "tensor"),
        P("rollout"),
        P(),
    )
    return jax.shard_map(
        body, mesh=mesh, in_specs=placed, out_specs=P(None, "rollout", "tensor"), check_vma=False
    )
```

```python
import functools
import math

import jax
import jax.numpy as jnp
from jax import lax
from jax.experimental import pallas as pl
from jax.experimental.pallas import tpu as pltpu
from jax.sharding import PartitionSpec as P

MESH = pl.DeviceIdType.MESH
HD = 128
STEPS = 4
ROWS = 128
TOK = STEPS * ROWS
D = 8192
PART = 1024
SUB = 256
RANK = 64
HALF = RANK // 2
QW = 512
KW = 128
QFULL = 4096
KFULL = 1024
NSEM = 190
CROSS = (512, 640)
BF = jnp.bfloat16
F32 = jnp.float32


ORDER = [
    ("f_core", 1), ("c_tables", 0), ("f_core", 0), ("f_core", 2), ("f_core", 3), ("zu", 2),
    ("zd", 2), ("xx", 2), ("c_tables", 1), ("c_tables", 2), ("f_second", 1), ("c_tables", 3),
    ("c_split", 0), ("zu", 3), ("zd", 3), ("xx", 3), ("c_split", 1), ("c_split", 2),
    ("f_second", 0), ("c_split", 3), ("zu", 4), ("zd", 4), ("xx", 4), ("f_second", 2), ("zu", 5),
    ("zd", 5), ("xx", 5), ("f_second", 3), ("zu", 6), ("zd", 6), ("xx", 6), ("f_third", 1),
    ("f_third", 0), ("f_third", 2), ("xx", 7), ("f_third", 3), ("zu", 7), ("zd", 7), ("f_ra", 0),
    ("f_ra", 1), ("zu", 8), ("f_ra", 2), ("zd", 8), ("xx", 8), ("zu", 9), ("zd", 9), ("xx", 9),
    ("f_ra", 3), ("f_rb", 1), ("f_rb", 0), ("f_rb", 2), ("zu", 10), ("zd", 10), ("xx", 10),
    ("zu", 11), ("zd", 11), ("xx", 11), ("f_rb", 3), ("f_sb", 1), ("f_sb", 2), ("xx", 12),
    ("xx", 13), ("zu", 12), ("zd", 12), ("f_sb", 3), ("f_sa", 1), ("xx", 14), ("zu", 13),
    ("zd", 13), ("f_sa", 2), ("xx", 15), ("c_merge_q", 0), ("xx", 16), ("zu", 14), ("zd", 14),
    ("f_sa", 3), ("zu", 15), ("zu", 16), ("zd", 15), ("zd", 16), ("xx", 17), ("xx", 18), ("zu", 17),
    ("zd", 17), ("xx", 19), ("xx", 20), ("xx", 21), ("xx", 22), ("f_yf", 1), ("xx", 23),
    ("c_merge_kv", 0), ("zu", 18), ("zd", 18), ("xx", 24), ("zu", 19), ("zd", 19), ("xx", 25),
    ("zu", 20), ("zd", 20), ("xx", 26), ("c_merge_q", 1), ("c_merge_q", 2), ("f_yf", 2), ("zu", 21),
    ("zd", 21), ("xx", 27), ("xx", 28), ("zu", 22), ("zd", 22), ("xx", 29), ("f_yf", 3), ("zu", 23),
    ("zd", 23), ("xx", 30), ("f_last", 1), ("c_merge_kv", 1), ("xx", 31), ("c_merge_kv", 2),
    ("c_most", 0), ("c_most", 1), ("f_last", 2), ("c_merge_q", 3), ("x_end", 0), ("x_end", 1),
    ("c_most", 2), ("f_last", 3), ("c_most", 3), ("c_most", 4), ("c_most", 5), ("c_merge_kv", 3),
    ("c_most", 6), ("c_rest", 0), ("c_rest", 1), ("c_rest", 2), ("c_rest", 3), ("c_rest", 4),
    ("c_rest", 5), ("c_rest", 6), ("x_end", 2), ("c_most", 7), ("c_rest", 7),
]


def coordinates():
    rollout = lax.axis_index("rollout")
    tensor = lax.axis_index("tensor")
    core = rollout % 2
    x = (tensor // 4) * 2 + (rollout // 2) % 2
    return core, x, rollout // 4, tensor % 4


def device(core, x, y, z):
    return ((y * 2 + x % 2) * 2 + core, (x // 2) * 4 + z)


def decode(
    owners_ref,
    x_hbm,
    wq_hbm,
    wkv_hbm,
    down_hbm,
    up_hbm,
    bq_ref,
    bkv_ref,
    len_ref,
    rows_ref,
    cache_hbm,
    o_ref,
    q_ref,
    k_ref,
    v_ref,
    cache_ref,
    recent,
    recent_probs,
    probs,
    xs,
    wq,
    wkv,
    mkv,
    pairs,
    upstage,
    held,
    rcore,
    csum,
    ry,
    yq,
    rz,
    rx,
    fac,
    ru,
    uall,
    upkv,
    acc,
    cos_ref,
    sin_ref,
    send,
    recv,
    local,
):
    core, x, y, z = coordinates()
    tensor = (x // 2) * 4 + z
    me = ((y * 2 + x % 2) * 2 + core) * 8 + tensor

    def at(dc=0, dx=0, dy=0, dz=0):
        return device((core + dc) % 2, (x + dx) % 4, (y + dy) % 4, (z + dz) % 4)

    z_up, z_down, z_far = at(dz=1), at(dz=3), at(dz=2)
    x_far = at(dx=2)
    y_up, y_down = at(dy=1), at(dy=3)
    other = at(dc=1)
    y_all = [at(dc=c, dy=d) for c in range(2) for d in range(4) if c + d > 0]
    partners = [z_up, z_down, z_far, at(dx=1), x_far, at(dx=3), *y_all]

    locals_used = [0]

    def fetch(src, dst):
        copy = pltpu.make_async_copy(src, dst, local.at[locals_used[0]])
        locals_used[0] += 1
        copy.start()
        return copy

    mine = pl.multiple_of(core * HALF, HALF)
    theirs = pl.multiple_of((1 - core) * HALF, HALF)
    rows = pl.ds(mine, HALF)

    barrier = pltpu.get_barrier_semaphore()
    for partner in partners:
        pl.semaphore_signal(barrier, inc=1, device_id=partner, device_id_type=MESH)
    ups = []
    for t in range(8):
        ups.append(fetch(up_hbm.at[0, :, pl.ds(t * QW, QW)], upstage.at[:, pl.ds(t * PART, QW)]))
        for j in range(2):
            ups.append(
                fetch(
                    up_hbm.at[0, :, pl.ds(QFULL + j * KFULL + t * KW, KW)],
                    upstage.at[:, pl.ds(t * PART + QW + j * KW, KW)],
                )
            )
    down_load = fetch(down_hbm.at[0, :, rows], held)
    for t in range(8):
        upstage[:, pl.ds(t * PART + QW + 2 * KW, PART - QW - 2 * KW)] = jnp.zeros(
            (RANK, PART - QW - 2 * KW), BF
        )
    pl.semaphore_wait(barrier, len(partners))

    used = [0]

    def put(src, dst, target):
        index = used[0]
        used[0] += 1
        copy = pltpu.make_async_remote_copy(
            src_ref=src,
            dst_ref=dst,
            send_sem=send.at[index],
            recv_sem=recv.at[index],
            device_id=target,
            device_id_type=MESH,
        )
        copy.start()
        return copy

    started = []
    arrived = set()

    def land(copy):
        if id(copy) not in arrived:
            arrived.add(id(copy))
            copy.wait_recv()

    def push(src, target, dst=None):
        copy = put(src, src if dst is None else dst, target)
        started.append(copy)
        return copy

    def chunk(t, p, columns=(0, PART)):
        piece = xs.at[t, p // 2, pl.ds((p % 2) * 64, 64)]
        if columns == (0, PART):
            return piece
        return piece.at[:, pl.ds(columns[0], columns[1] - columns[0])]

    def own(p):
        return x_hbm.at[p // 2, pl.ds((p % 2) * 64, 64)]

    base = (x // 2) * 4
    far_base = 4 - base
    far_slot = far_base + z
    z_prev, z_next, z_opp = (z + 3) % 4, (z + 1) % 4, (z + 2) % 4

    def across(member):
        return push(down_hbm.at[0, member - 1, pl.ds(theirs, HALF)], other, rcore.at[member])

    core_copies = {1: across(1)}

    got = {}

    def near_part(p):
        return (0, CROSS[p % 2])

    def far_part(p):
        return (CROSS[p % 2], PART)

    up_list = [("own", p) for p in range(8)]
    up_list += [("far", p) for p in range(4)] + [("ring", p) for p in range(4)]
    up_list += [("far", p) for p in range(4, 8)] + [("farring", p) for p in range(4)]

    def z_send(direction, i):
        kind, p = up_list[i]
        if direction < 0:
            p = (p + 4) % 8
        target, behind = (z_up, z_prev) if direction > 0 else (z_down, z_next)
        if kind == "own":
            copy = push(own(p), target, chunk(tensor, p))
        elif kind == "far":
            land(got["x", p])
            copy = push(chunk(far_slot, p, near_part(p)), target)
        elif kind == "ring":
            land(got[direction, "own", p])
            copy = push(chunk(base + behind, p), target)
        else:
            land(got[direction, "far", p])
            copy = push(chunk(far_base + behind, p, near_part(p)), target)
        got[direction, kind, p] = copy

    def zu(i):
        z_send(1, i)

    def zd(i):
        z_send(-1, i)

    x_list = [("own", p) for p in (0, 4, 1, 5, 2, 6, 3, 7)]
    for p in range(4):
        x_list += [("prev", p), ("next", p + 4)]
    for p in range(4):
        x_list += [("prev", p + 4), ("next", p)]
    for p in range(4):
        x_list += [("opp", p), ("opp", p + 4)]

    def xx(i):
        kind, p = x_list[i]
        if kind == "own":
            got["x", p] = push(own(p), x_far, chunk(tensor, p))
            return
        if kind == "prev":
            slot, arrival = base + z_prev, got[1, "own", p]
        elif kind == "next":
            slot, arrival = base + z_next, got[-1, "own", p]
        else:
            slot, arrival = base + z_opp, got[1 if p < 4 else -1, "ring", p]
        land(arrival)
        got["x", kind, p] = push(chunk(slot, p, far_part(p)), x_far)

    def x_end(part):
        for p in range(8):
            if part == 0:
                land(got["x", "prev", p])
                land(got[1, "far", p])
            elif part == 1:
                land(got["x", "next", p])
                land(got[-1, "far", p])
            else:
                land(got["x", "opp", p])
                land(got[1 if p < 4 else -1, "farring", p])

    for i in range(2):
        zu(i)
        zd(i)
        xx(i)
    for copy in ups:
        copy.wait()
    core_copies[0] = push(upstage.at[pl.ds(theirs, HALF)], other, rcore.at[0])
    for member in (2, 3):
        core_copies[member] = across(member)
    x_load = fetch(x_hbm, xs.at[tensor])
    wkv_load = fetch(wkv_hbm, wkv)
    wq_load = fetch(wq_hbm, wq)
    cache_load = fetch(cache_hbm, cache_ref)
    down_load.wait()

    def c_tables(s):
        lane = lax.broadcasted_iota(jnp.int32, (ROWS, HD), 1)
        frequency = jnp.exp(
            -((lane % (HD // 2)).astype(F32) * (2.0 / HD)) * math.log(1000000.0)
        )
        lengths = jnp.broadcast_to(len_ref[...], (ROWS, HD)).astype(F32).T
        sign = jnp.where(lane < HD // 2, -1.0, 1.0)
        angles = (lengths + float(s)) * frequency
        cos_ref[pl.ds(s * ROWS, ROWS), :] = jnp.cos(angles)
        sin_ref[pl.ds(s * ROWS, ROWS), :] = jnp.sin(angles) * sign

    me_other = ((y * 2 + x % 2) * 2 + 1 - core) * 8 + tensor
    keep = [(owners_ref[m] == me).astype(F32).astype(BF) for m in range(3)]
    take = [(owners_ref[m] == me_other).astype(F32).astype(BF) for m in range(3)]

    def quarter(q):
        return pl.ds(pl.multiple_of(q * 2048, 2048), 2048)

    y_opp, y_next, y_prev = (y + 2) % 4, (y + 1) % 4, (y + 3) % 4
    low_rows, high_rows = pl.ds(0, HALF // 2), pl.ds(HALF // 2, HALF // 2)
    fac_low = pl.ds(mine, HALF // 2)
    fac_high = pl.ds(pl.multiple_of(mine + HALF // 2, HALF // 2), HALF // 2)
    state = {}

    def f_core(m):
        land(core_copies[m])

        def add_block(t, carry):
            start = pl.multiple_of(t * PART, PART)
            block = t if m > 0 else (t % 4) * 2 + t // 4
            place = pl.multiple_of(block * SUB, SUB)
            for q in range(4):
                if m > 0:
                    spans = [(m - 1, 0, SUB)]
                elif q < 2:
                    spans = [(0, 0, SUB)]
                else:
                    spans = [(1, 0, KW), (2, KW, KW)]
                for owner, offset, width in spans:
                    target = pl.ds(place + q * 2048 + offset, width)
                    if m == 0 and q == 3:
                        csum[m, :, target] = jnp.zeros((HALF, width), BF)
                        continue
                    columns = pl.ds(start + q * SUB + offset, width)
                    here = upstage[rows, columns] if m == 0 else held[m - 1, :, columns]
                    csum[m, :, target] = here * keep[owner] + rcore[m, :, columns] * take[owner]
            return carry

        lax.fori_loop(0, 8, add_block, 0)
        state["first", m] = [
            push(csum.at[m, low_rows, quarter(y_opp)], y_up, ry.at[m, 0]),
            push(csum.at[m, high_rows, quarter(y_opp)], y_down, ry.at[m, 1]),
        ]
        state["raw", m] = [
            push(csum.at[m, low_rows, quarter(y_prev)], y_down, ry.at[m, 2]),
            push(csum.at[m, high_rows, quarter(y_next)], y_up, ry.at[m, 3]),
        ]

    def f_second(m):
        land(state["first", m][0])
        ry[m, 0] = ry[m, 0] + csum[m, low_rows, quarter(y_next)]
        state["raw", m].append(push(ry.at[m, 0], y_up, ry.at[m, 4]))
        land(state["first", m][1])
        ry[m, 1] = ry[m, 1] + csum[m, high_rows, quarter(y_prev)]
        state["raw", m].append(push(ry.at[m, 1], y_down, ry.at[m, 5]))

    def wait_all(copies):
        for copy in copies:
            land(copy)

    def first_at(m, d):
        return at(dz=d) if m % 2 == 0 else at(dx=d)

    def second_at(m, d):
        return at(dx=d) if m % 2 == 0 else at(dz=d)

    def places(m):
        return (z, x) if m % 2 == 0 else (x, z)

    def wide(index):
        return pl.ds(pl.multiple_of(index * 512, 512), 512)

    def narrow(index):
        return pl.ds(pl.multiple_of(index * 128, 128), 128)

    def half_of(xx):
        return pl.ds(pl.multiple_of((xx // 2) * SUB, SUB), SUB)

    def f_third(m):
        wait_all(state["raw", m])
        yq[m, low_rows] = csum[m, low_rows, quarter(y)] + ry[m, 2] + ry[m, 4]
        yq[m, high_rows] = csum[m, high_rows, quarter(y)] + ry[m, 3] + ry[m, 5]
        outer = places(m)[0]
        state["ra", m] = [
            push(yq.at[m, :, wide((outer + d) % 4)], first_at(m, d), rz.at[m, d - 1])
            for d in (1, 2, 3)
        ]

    def f_ra(m):
        wait_all(state["ra", m])
        outer, inner = places(m)
        rz[m, 3] = yq[m, :, wide(outer)] + rz[m, 0] + rz[m, 1] + rz[m, 2]
        if m == 0:
            state["rb", m] = [
                push(rz.at[m, 3, :, half_of((x + d) % 4)], at(dx=d), ru.at[d - 1]) for d in (1, 2, 3)
            ]
            return
        state["rb", m] = [
            push(rz.at[m, 3, :, narrow((inner + d) % 4)], second_at(m, d), rx.at[m, d - 1])
            for d in (1, 2, 3)
        ]

    def f_rb(m):
        wait_all(state["rb", m])
        if m == 0:
            ru[3] = rz[m, 3, :, half_of(x)] + ru[0] + ru[1] + ru[2]
            place = uall.at[rows, pl.ds(pl.multiple_of(y * SUB, SUB), SUB)]
            state["u"] = [push(ru.at[3], device_id, place) for device_id in y_all]
            uall[rows, pl.ds(pl.multiple_of(y * SUB, SUB), SUB)] = ru[3]
            return
        outer, inner = places(m)
        rx[m, 3] = rz[m, 3, :, narrow(inner)] + rx[m, 0] + rx[m, 1] + rx[m, 2]
        span = pl.ds(pl.multiple_of(y * 2048 + outer * 512 + inner * 128, 128), 128)
        state["sb", m] = [
            push(rx.at[m, 3], second_at(m, d), fac.at[m, rows, span]) for d in (1, 2, 3)
        ]
        fac[m, rows, span] = rx[m, 3]

    def f_sb(m):
        wait_all(state["sb", m])
        outer = places(m)[0]
        piece = fac.at[m, rows, pl.ds(pl.multiple_of(y * 2048 + outer * 512, 512), 512)]
        state["sa", m] = [push(piece, first_at(m, d)) for d in (1, 2, 3)]

    def f_sa(m):
        wait_all(state["sa", m])
        piece = fac.at[m, rows, quarter(y)]
        state["ys", m] = [push(piece, y_up), push(piece, y_down), push(piece, other)]

    def f_yf(m):
        land(state["ys", m][0])
        up = push(fac.at[m, fac_low, quarter(y_prev)], y_up)
        down_core = push(fac.at[m, rows, quarter(y_prev)], other)
        land(state["ys", m][1])
        down = push(fac.at[m, fac_high, quarter(y_next)], y_down)
        up_core = push(fac.at[m, rows, quarter(y_next)], other)
        state["yf", m] = [up, down, down_core, up_core]

    def f_last(m):
        wait_all(state["yf", m][:2])
        state["yl", m] = push(fac.at[m, rows, quarter(y_opp)], other)

    def whole(part, m):
        if part == 0:
            land(state["ys", m][2])
        elif part < 3:
            land(state["yf", m][1 + part])
        else:
            land(state["yl", m])

    def c_split(part):
        if part == 0:
            wkv_load.wait()

        def split_pairs(i, carry):
            pairs[...] = wkv[pl.ds(pl.multiple_of(i * 1024, 1024), 1024), :].astype(F32)
            ks = pl.ds(pl.multiple_of(i * 512, 512), 512)
            for j in range(2):
                mkv[ks, pl.ds(j * KW, KW)] = pairs[pl.ds(j, 512, stride=2), :].astype(BF)
            return carry

        lax.fori_loop(part * 4, part * 4 + 4, split_pairs, 0)

    quarters = [y, y_prev, y_next, y_opp]

    def merge_rows(part, t):
        spot = pl.ds(pl.multiple_of(quarters[part] * 2048 + t * SUB, SUB), SUB)
        return spot, pl.ds(pl.multiple_of(t * PART + quarters[part] * SUB, SUB), SUB)

    def c_merge_q(part):
        wait_all(state["u"])
        whole(part, 1)
        if part == 0:
            wq_load.wait()

        def merge(t, carry):
            spot, ks = merge_rows(part, t)
            low = lax.dot_general(
                fac[1, :, spot], uall[:, pl.ds(0, QW)], (((0,), (0,)), ((), ())), preferred_element_type=F32
            )
            wq[ks, :] = (wq[ks, :].astype(F32) + low).astype(BF)
            return carry

        lax.fori_loop(0, 8, merge, 0)

    def c_merge_kv(part):
        wait_all(state["u"])
        for m in (2, 3):
            whole(part, m)
        if part == 0:
            upkv[...] = jnp.zeros_like(upkv)
            for j in range(2):
                upkv[pl.ds(j * RANK, RANK), pl.ds(j * KW, KW)] = uall[:, pl.ds(QW + j * KW, KW)]

        def merge(t, carry):
            spot, ks = merge_rows(part, t)
            low = lax.dot_general(
                fac[pl.ds(2, 2), :, spot].reshape(2 * RANK, SUB),
                upkv[...],
                (((0,), (0,)), ((), ())),
                preferred_element_type=F32,
            )
            mkv[ks, :] = (mkv[ks, :].astype(F32) + low).astype(BF)
            return carry

        lax.fori_loop(0, 8, merge, 0)

    sources = [
        tensor, base + z_prev, base + z_next, base + z_opp,
        far_slot, far_base + z_prev, far_base + z_next, far_base + z_opp,
    ]

    def project(i, parts, first=False):
        t = sources[i]
        query = keyval = None
        for part in parts:
            features = pl.ds(pl.multiple_of(quarters[part] * SUB, SUB), SUB)
            ks = pl.ds(pl.multiple_of(t * PART + quarters[part] * SUB, SUB), SUB)
            received = xs[t, :, :, features].reshape(TOK, SUB)
            more_query = jnp.dot(received, wq[ks, :], preferred_element_type=F32)
            more_keyval = jnp.dot(received, mkv[ks, :], preferred_element_type=F32)
            query = more_query if query is None else query + more_query
            keyval = more_keyval if keyval is None else keyval + more_keyval
        if first:
            acc[:, pl.ds(0, QW)] = query
            acc[:, pl.ds(QW, 2 * KW)] = keyval
        else:
            acc[:, pl.ds(0, QW)] += query
            acc[:, pl.ds(QW, 2 * KW)] += keyval

    def c_most(i):
        if i == 0:
            x_load.wait()
        project(i, (0, 1, 2), i == 0)

    def c_rest(i):
        project(i, (3,))

    steps = dict(
        f_core=f_core, f_second=f_second, f_third=f_third, f_ra=f_ra, f_rb=f_rb, f_sb=f_sb, f_sa=f_sa,
        f_yf=f_yf, f_last=f_last,
        zu=zu, zd=zd, xx=xx, x_end=x_end, c_tables=c_tables, c_split=c_split, c_merge_q=c_merge_q, c_merge_kv=c_merge_kv,
        c_most=c_most, c_rest=c_rest,
    )
    for name, index in ORDER:
        steps[name](index)

    def rotate(vectors, token_rows):
        return vectors * cos_ref[token_rows, :] + pltpu.roll(vectors, HD // 2, 1) * sin_ref[token_rows, :]

    for s in range(STEPS):
        token_rows = pl.ds(s * ROWS, ROWS)
        for h in range(QW // HD):
            columns = pl.ds(h * HD, HD)
            turned = rotate(acc[token_rows, columns] + bq_ref[:, columns], token_rows)
            q_ref[:, s * 4 + h, :] = turned.astype(BF).astype(F32)
        turned = rotate(acc[token_rows, pl.ds(QW, KW)] + bkv_ref[pl.ds(0, 1), :], token_rows)
        k_ref[s] = turned.astype(BF)
        v_ref[s] = (acc[token_rows, pl.ds(QW + KW, KW)] + bkv_ref[pl.ds(1, 1), :]).astype(BF)

    cache_load.wait()

    def attend_block(i, carry):
        attend(
            pl.multiple_of(i * BLOCK, BLOCK), rows_ref, q_ref, k_ref, v_ref, cache_ref, o_ref,
            recent, recent_probs, probs,
        )
        return carry

    lax.fori_loop(0, ROWS // BLOCK, attend_block, 0)
    for copy in started:
        land(copy)
        copy.wait_send()


BLOCK = 32


def attend(first, len_ref, q_ref, k_ref, v_ref, cache_ref, o_ref, recent, recent_probs, probs):
    rows = pl.ds(first, BLOCK)
    queries = q_ref[rows].reshape(BLOCK * 16, HD).astype(BF)
    keys = k_ref[:, rows, :].reshape(BLOCK * STEPS, HD)
    scale = 1.0 / math.sqrt(HD)
    scores = (
        lax.dot_general(queries, keys, (((1,), (1,)), ((), ())), preferred_element_type=F32) * scale
    )
    row = lax.broadcasted_iota(jnp.int32, scores.shape, 0)
    lane = lax.broadcasted_iota(jnp.int32, scores.shape, 1)
    valid = (row // 16 == lane % BLOCK) & (lane // BLOCK <= (row // 4) % 4)
    recent[...] = jnp.where(valid, scores, -1e30)
    slots = lax.broadcasted_iota(jnp.int32, (16, HD), 1)
    for r in range(0, BLOCK, 2):
        pair = pl.ds(first + r, 2)
        raw = lax.dot_general(
            q_ref[pair].reshape(32, HD).astype(BF),
            cache_ref[0, pair].reshape(2 * HD, HD),
            (((1,), (1,)), ((), ())),
            preferred_element_type=F32,
        )
        for j in range(2):
            mine = raw[16 * j : 16 * j + 16, HD * j : HD * j + HD]
            q_ref[first + r + j] = jnp.where(slots < len_ref[first + r + j], mine * scale, -1e30)
    for part in range(4):
        group = pl.ds(first + part * BLOCK // 4, BLOCK // 4)
        mine = pl.ds(part * BLOCK * 4, BLOCK * 4)
        cached = q_ref[group].reshape(BLOCK * 4, HD)
        fresh = recent[mine, :]
        top = jnp.max(jnp.maximum(cached, fresh), axis=1, keepdims=True)
        cached = jnp.exp(cached - top)
        fresh = jnp.exp(fresh - top)
        total = jnp.sum(cached + fresh, axis=1, keepdims=True)
        recent_probs[mine, :] = (fresh / total).astype(BF)
        probs[mine, :] = (cached / total).astype(BF)
    for r in range(0, BLOCK, 2):
        both = jnp.concatenate([cache_ref[1, first + r], cache_ref[1, first + r + 1]], axis=1)
        raw = jnp.dot(probs[pl.ds(r * 16, 32), :], both, preferred_element_type=F32)
        for j in range(2):
            q_ref[first + r + j] = raw[16 * j : 16 * j + 16, HD * j : HD * j + HD]
    values = v_ref[:, rows, :].reshape(BLOCK * STEPS, HD)
    q_ref[rows] += jnp.dot(recent_probs[...], values, preferred_element_type=F32).reshape(
        BLOCK, 16, HD
    )
    for s in range(STEPS):
        for h in range(4):
            o_ref[s, rows, pl.ds(h * HD, HD)] = q_ref[rows, s * 4 + h, :].astype(BF)


def body(
    inputs,
    w_query,
    w_keyval,
    bias_query,
    bias_keyval,
    factor_down,
    factor_up,
    cache,
    lengths,
    owners,
):
    any_space = pl.BlockSpec(memory_space=pl.ANY)
    vmem = pl.BlockSpec(memory_space=pltpu.VMEM)
    smem = pl.BlockSpec(memory_space=pltpu.SMEM)
    return pl.pallas_call(
        decode,
        out_shape=jax.ShapeDtypeStruct((STEPS, ROWS, QW), BF),
        in_specs=[smem] + [any_space] * 5 + [vmem] * 3 + [smem, any_space],
        out_specs=vmem,
        scratch_shapes=[
            pltpu.VMEM((ROWS, 16, HD), F32),
            pltpu.VMEM((STEPS, ROWS, HD), BF),
            pltpu.VMEM((STEPS, ROWS, HD), BF),
            pltpu.VMEM((2, ROWS, HD, HD), BF),
            pltpu.VMEM((BLOCK * 16, HD), F32),
            pltpu.VMEM((BLOCK * 16, HD), BF),
            pltpu.VMEM((BLOCK * 16, HD), BF),
            pltpu.VMEM((8, STEPS, ROWS, PART), BF),
            pltpu.VMEM((D, QW), BF),
            pltpu.VMEM((2 * D, KW), BF),
            pltpu.VMEM((D, 2 * KW), BF),
            pltpu.VMEM((1024, KW), F32),
            pltpu.VMEM((RANK, D), BF),
            pltpu.VMEM((3, HALF, D), BF),
            pltpu.VMEM((4, HALF, D), BF),
            pltpu.VMEM((4, HALF, D), BF),
            pltpu.VMEM((4, 6, HALF // 2, 2048), BF),
            pltpu.VMEM((4, HALF, 2048), BF),
            pltpu.VMEM((4, 4, HALF, 512), BF),
            pltpu.VMEM((4, 4, HALF, 128), BF),
            pltpu.VMEM((4, RANK, D), BF),
            pltpu.VMEM((4, HALF, SUB), BF),
            pltpu.VMEM((RANK, PART), BF),
            pltpu.VMEM((2 * RANK, 2 * KW), BF),
            pltpu.VMEM((TOK, QW + 2 * KW), F32),
            pltpu.VMEM((TOK, HD), F32),
            pltpu.VMEM((TOK, HD), F32),
            pltpu.SemaphoreType.DMA((NSEM,)),
            pltpu.SemaphoreType.DMA((NSEM,)),
            pltpu.SemaphoreType.DMA((32,)),
        ],
        compiler_params=pltpu.CompilerParams(
            collective_id=0, has_side_effects=True, vmem_limit_bytes=58 << 20
        ),
    )(
        owners,
        inputs,
        w_query,
        w_keyval.reshape(2 * D, KW),
        factor_down,
        factor_up,
        bias_query.reshape(1, QW),
        bias_keyval,
        lengths.reshape(1, ROWS),
        lengths,
        cache,
    )


def solution(mesh):
    placed = (
        P(None, "rollout", "tensor"),
        P(None, "tensor"),
        P(None, None, "tensor"),
        P("tensor"),
        P(None, "tensor"),
        P(("rollout", "tensor"), None, None, None),
        P(("rollout", "tensor"), None, None),
        P(None, "rollout", None, "tensor"),
        P("rollout"),
        P(),
    )
    return jax.shard_map(
        body, mesh=mesh, in_specs=placed, out_specs=P(None, "rollout", "tensor"), check_vma=False
    )
```
